128 devices in a mesh: site: 2 (over core), sector: 64 (over z, x, y).
Axes of the slice: x: 4, y: 4, z: 4, core: 2. Of those that a mesh axis runs over, the one named last changes fastest.
Arguments:
- environment: bfloat16 [256, 128, 30, 128], P('sector'), may hold values from -6 to 6
- amplitudes: bfloat16 [2, 256, 4, 128, 128], P('site', 'sector'), may hold values from -0.5 to 0.5
- mpo_weight: bfloat16 [2, 30, 4, 4, 30], P('site'), may hold values from -0.75 to 0.75
- mpo_mask: int32 [2, 30, 30], P('site'), may hold values 0 or 1
- sector_count: int32 [64], replicated, may hold values from 1 to 4, as said below
Outputs:
- env_out: bfloat16 [2, 256, 128, 30, 128], P('site', 'sector')
The draws below stay inside these ranges and needn't reach their ends.
Inputs may be any that keep to these rules, and one draw needn't show every extreme that they name: `sector_count`: every owner holds one or more sectors and some owner holds 4; owner 64 - 2 holds exactly one sector.
All inputs are finite; a program needn't handle non-finite values. No bound on the sum of `mpo_mask` on one device may be relied on, other than what follows from the above.
Results may differ from the reference program's by a relative error of at most 0.017.
Values may be sent and summed in bfloat16 or wider, within the bound.
No kernel may reach another device: no remote copies, remote signals or barrier semaphores. Data moves between devices by JAX's collectives and lax.ppermute only.
A program may use at most 128 MiB of HBM per device.

```python
import jax
import jax.numpy as jnp
from jax import lax

S = 128
W = 30
PHYS = 4
KD = 2
MAXB = 4
KS = 256
N_SITE = 2
N_SECTOR = 64


def draw_sector_count(key, part):
    key = jax.random.fold_in(key, 11)
    key_rot, key_diff, key_flip = jax.random.split(key, 3)
    owner_ids = jnp.arange(N_SECTOR, dtype=jnp.int32)
    rotation = jax.random.randint(key_rot, (), 0, 3, dtype=jnp.int32)
    triple = jnp.array([2 * KD, 1, KD - 1], jnp.int32)
    first_counts = triple[(owner_ids + rotation) % 3]
    middle = owner_ids - 3
    pair_ids = jnp.maximum(middle, 0) // 2
    within = jnp.maximum(middle, 0) % 2
    differences = jax.random.randint(key_diff, (N_SECTOR,), 0, KD, dtype=jnp.int32)
    flips = jax.random.randint(key_flip, (N_SECTOR,), 0, 2, dtype=jnp.int32)
    signs = 1 - 2 * ((within + flips[pair_ids]) % 2)
    middle_counts = KD + differences[pair_ids] * signs
    if (N_SECTOR - 5) % 2 == 1:
        middle_counts = jnp.where(middle == N_SECTOR - 6, KD, middle_counts)
    top_counts = jnp.where(owner_ids == N_SECTOR - 2, 1, 2 * KD - 1)
    counts = jnp.where(owner_ids < 3, first_counts, jnp.where(owner_ids >= N_SECTOR - 2, top_counts, middle_counts))
    return counts.astype(jnp.int32)


def touch_ends(values, rng, least, top_value):
    longest = values.shape.index(max(values.shape))
    spots = []
    for shift in (0, 1):
        where = [jax.random.randint(jax.random.fold_in(rng, axis), (), 0, length) for axis, length in enumerate(values.shape)]
        where[longest] = (where[longest] + shift) % values.shape[longest]
        spots.append(tuple(where))
    return values.at[spots[0]].set(least).at[spots[1]].set(top_value)


def steps_of(key, shape, cuts, low, top_value):
    def one(axis_at, parts):
        draws = jax.random.uniform(jax.random.fold_in(jax.random.fold_in(key, 6), axis_at), (parts,), jnp.float32, low / len(cuts), top_value / len(cuts))
        return jnp.repeat(jnp.exp(draws), shape[axis_at] // parts).reshape((-1,) + (1,) * (len(shape) - axis_at - 1))

    loudness = one(*cuts[0])
    for cut in cuts[1:]:
        loudness = loudness * one(*cut)
    return loudness


def gaussian(key, extent, scale, limit, shards=(), kind=jnp.bfloat16):
    entries = jax.random.normal(key, extent, jnp.float32) * scale
    if len(shards) > 0:
        entries = steps_of(key, extent, shards, -0.22, 0.18) * entries
    return jnp.clip(entries, min=-limit, max=limit).astype(kind)


def setup_inputs(seed: int = 0) -> dict:
    splits = jax.random.split(jax.random.key(seed), 6)
    return {
        "environment": gaussian(splits[0], (KS, S, W, S), 1.0, 6.0, ((0, 64),)),
        "amplitudes": gaussian(splits[1], (N_SITE, KS, PHYS, S, S), S ** -0.5, 0.5, ((0, 2), (1, 64))),
        "mpo_weight": gaussian(splits[2], (N_SITE, W, PHYS, PHYS, W), (2 * W) ** -0.5, 0.75, ((0, 2),)),
        "mpo_mask": touch_ends((jax.random.randint(splits[3], (N_SITE, W, W), 0, 2) < 1).astype(jnp.int32), jax.random.fold_in(splits[3], 1), 0, 1),
        "sector_count": draw_sector_count(jax.random.fold_in(splits[5], 71), 0),
    }


def mpo_effective(mpo_site, mask_site):
    charges = jnp.array([0, 1, 1, 2], jnp.int32)
    neutral = (charges[:, None] == charges[None, :]).astype(jnp.float32)
    keep_mask = mask_site.astype(jnp.float32)[:, None, None, :] * neutral[None, :, :, None]
    return (mpo_site.astype(jnp.float32) * keep_mask).astype(jnp.bfloat16)


def sector_terms(env_block, amp_block, mpo_eff):
    contracted = jnp.einsum('awc,tcb->awtb', env_block.astype(jnp.float32), amp_block.astype(jnp.float32)).astype(jnp.bfloat16)
    with_mpo = jnp.einsum('awtb,wstv->asvb', contracted.astype(jnp.float32), mpo_eff.astype(jnp.float32)).astype(jnp.bfloat16)

    def project(start_class, stop_class):
        return jnp.einsum('sab,asvc->bvc', amp_block[start_class:stop_class].astype(jnp.float32), with_mpo[:, start_class:stop_class].astype(jnp.float32)).astype(jnp.bfloat16)

    return project(0, 1), project(1, 3), project(3, 4)


def reference(environment, amplitudes, mpo_weight, mpo_mask, sector_count):
    starts = (jnp.cumsum(sector_count) - sector_count).astype(jnp.int32)
    sector_ids = jnp.arange(KD * N_SECTOR, dtype=jnp.int32)
    owners = jnp.sum((starts[None, 1:] <= sector_ids[:, None]).astype(jnp.int32), axis=1).astype(jnp.int32)
    slot_of = (owners * MAXB + sector_ids - starts[owners]).astype(jnp.int32)
    current = environment[slot_of]
    outputs = []
    for site_index in range(N_SITE):
        mpo_eff = mpo_effective(mpo_weight[site_index], mpo_mask[site_index])
        amp_sectors = amplitudes[site_index][slot_of]

        def one_sector(inputs_pair):
            return sector_terms(inputs_pair[0], inputs_pair[1], mpo_eff)

        zero_p, one_p, two_p = lax.map(one_sector, (current, amp_sectors))
        zero_block = jnp.zeros_like(one_p[:1]).astype(jnp.float32)
        summed = zero_p.astype(jnp.float32)
        summed = summed + jnp.concatenate([zero_block, one_p[:-1].astype(jnp.float32)], 0)
        summed = summed + jnp.concatenate([zero_block, zero_block, two_p[:-2].astype(jnp.float32)], 0)
        current = summed.astype(jnp.bfloat16)
        placed = jnp.zeros(environment.shape, jnp.bfloat16).at[slot_of].set(current)
        outputs.append(placed)
    return jnp.stack(outputs)
```

```python
import functools

import jax
import jax.numpy as jnp
from jax import lax
from jax.experimental import pallas as pl
from jax.experimental.pallas import tpu as pltpu
from jax.sharding import PartitionSpec as P

S = 128
W = 30
HALF = 15
PAIRS = ((0, 0), (1, 1), (1, 2), (2, 1), (2, 2), (3, 3))
AXES = ("site", "sector")
F32 = jnp.float32
BF16 = jnp.bfloat16
VMEM_LIMIT = 56 * 1024 * 1024


def iota(shape, dim):
    return lax.broadcasted_iota(jnp.int32, shape, dim)


def expand_operator(scal, site, split, states, w_own, w_oth, wk):
    core = scal[1]
    mine = (core == site).astype(F32)
    row_v = iota((8 * HALF, W), 0) // 8 + core * HALF
    pick_v = (row_v == iota((8 * HALF, W), 1)).astype(BF16)
    place = iota((W, 8 * W), 1) // 8
    if split:
        place = jnp.where(core == 0, place, jnp.where(place < HALF, place + HALF, place - HALF))
    pick_w = (place == iota((W, 8 * W), 0)).astype(BF16)
    diagonal = (iota((8 * HALF, 8 * W), 0) % 8) == (iota((8 * HALF, 8 * W), 1) % 8)
    for p, (s, s2) in enumerate(PAIRS):
        if s not in states:
            continue
        block = (w_own[p].astype(F32) * mine + w_oth[p].astype(F32) * (1.0 - mine)).astype(BF16)
        rows = lax.dot_general(pick_v, block, (((1,), (1,)), ((), ())), preferred_element_type=F32).astype(BF16)
        full = jnp.dot(rows, pick_w, preferred_element_type=F32)
        wk[p] = jnp.where(diagonal, full, 0.0).astype(BF16)


def pick_amp(scal, site, a_own, a_oth, s):
    mine = scal[1] == site
    return jnp.where(mine, a_own[0, s].astype(F32), a_oth[0, s].astype(F32)).astype(BF16)


def first_steps(left, amps, states, wk, z):
    columns = jnp.concatenate([amps[s] for s in states], axis=1) if len(states) > 1 else amps[states[0]]
    for g in range(8):
        block = left[:, 16 * g : 16 * g + 16, :].reshape(W * 16, S)
        c = jnp.dot(block, columns, preferred_element_type=F32)
        c = c.reshape(W, 16, S * len(states))
        low = c[:, :8, :].reshape(W * 8, S * len(states)).astype(BF16)
        high = c[:, 8:, :].reshape(W * 8, S * len(states)).astype(BF16)
        rights = [
            jnp.concatenate([low[:, S * k : S * k + S], high[:, S * k : S * k + S]], axis=1)
            for k in range(len(states))
        ]
        for s in states:
            total = None
            for p, (left_s, s2) in enumerate(PAIRS):
                if left_s == s:
                    term = jnp.dot(wk[p], rights[states.index(s2)], preferred_element_type=F32)
                    total = term if total is None else total + term
            total = total.reshape(HALF, 8, 2 * S)
            z[s, :, 16 * g : 16 * g + 16, :] = jnp.concatenate(
                [total[:, :, :S], total[:, :, S:]], axis=1
            ).astype(BF16)


def last_step(amps, states, z, sink):
    turned = [amps[s].astype(F32).T.astype(BF16) for s in states]
    lhs = jnp.concatenate(turned, axis=1) if len(states) > 1 else turned[0]
    for v in range(0, HALF, 2):
        count = min(2, HALF - v)
        rhs = jnp.concatenate(
            [jnp.concatenate([z[s, v + i] for s in states], axis=0) if len(states) > 1 else z[states[0], v + i] for i in range(count)],
            axis=1,
        ) if count > 1 else (jnp.concatenate([z[s, v] for s in states], axis=0) if len(states) > 1 else z[states[0], v])
        out = jnp.dot(lhs, rhs, preferred_element_type=F32)
        for i in range(count):
            sink(v + i, out[:, S * i : S * i + S])


def form_left(scal, slot, left, refs):
    mine, other, x_own, x_oth, y_own, y_oth = refs
    any_in = scal[2] > 0
    take_x = jnp.logical_and(slot == 0, any_in)
    take_y = jnp.logical_and(slot == 1, any_in)

    @pl.when(take_x)
    def _():
        left[:HALF] = (mine[0].astype(F32) + x_own[...].astype(F32)).astype(BF16)
        left[HALF:] = (other[0].astype(F32) + x_oth[...].astype(F32)).astype(BF16)

    @pl.when(take_y)
    def _():
        left[:HALF] = (mine[0].astype(F32) + y_own[...].astype(F32)).astype(BF16)
        left[HALF:] = (other[0].astype(F32) + y_oth[...].astype(F32)).astype(BF16)

    @pl.when(jnp.logical_not(jnp.logical_or(take_x, take_y)))
    def _():
        left[:HALF] = mine[0]
        left[HALF:] = other[0]


def y_kernel(site, scal, *refs):
    split = site == 1
    n_left = 6 if split else 1
    lefts, refs = refs[:n_left], refs[n_left:]
    a_own, a_oth, w_own, w_oth, out, left, wk, z = refs
    expand_operator(scal, site, split, (3,), w_own, w_oth, wk)
    amps = {3: pick_amp(scal, site, a_own, a_oth, 3)}
    if split:
        form_left(scal, scal[0] - 1, left, lefts)
        source = left
    else:
        source = lefts[0].at[0]
    first_steps(source, amps, (3,), wk, z)

    def sink(v, block):
        out[v] = block.astype(BF16)

    last_step(amps, (3,), z, sink)


def x_kernel(site, scal, *refs):
    split = site == 1
    n_left = 6 if split else 1
    lefts, refs = refs[:n_left], refs[n_left:]
    a_own, a_oth, w_own, w_oth, out, left, wk, z, acc = refs
    step = pl.program_id(0)
    count = scal[0]

    def source_of(slot):
        if split:
            form_left(scal, slot, left, lefts)
            return left
        return lefts[0].at[0]

    @pl.when(step == 0)
    def _():
        expand_operator(scal, site, split, (1, 2, 3), w_own, w_oth, wk)
        amps = {s: pick_amp(scal, site, a_own, a_oth, s) for s in (1, 2)}
        first_steps(source_of(count - 1), amps, (1, 2), wk, z)

        def sink(v, block):
            acc[v] = block

        last_step(amps, (1, 2), z, sink)

    @pl.when(jnp.logical_and(step == 1, count >= 2))
    def _():
        amps = {3: pick_amp(scal, site, a_own, a_oth, 3)}
        first_steps(source_of(count - 2), amps, (3,), wk, z)

        def sink(v, block):
            out[v] = (acc[v] + block).astype(BF16)

        last_step(amps, (3,), z, sink)

    @pl.when(jnp.logical_and(step == 1, count < 2))
    def _():
        out[...] = acc[...].astype(BF16)


def q_kernel(site, scal, *refs):
    split = site == 1
    n_left = 6 if split else 1
    lefts, refs = refs[:n_left], refs[n_left:]
    a_own, a_oth, w_own, w_oth, out, left, wk, z, next_one, next_two = refs
    step = pl.program_id(0)
    count = scal[0]
    source = left if split else lefts[0].at[0]

    @pl.when(step == 0)
    def _():
        expand_operator(scal, site, split, (0, 1, 2, 3), w_own, w_oth, wk)
        next_one[...] = jnp.zeros_like(next_one)
        next_two[...] = jnp.zeros_like(next_two)

    if split:
        @pl.when(step < count)
        def _():
            form_left(scal, step, left, lefts)

    def amps_of(states):
        return {s: pick_amp(scal, site, a_own, a_oth, s) for s in states}

    def sink_zero(v, block):
        out[0, v] = (block + next_one[v]).astype(BF16)

    def sink_one(v, block):
        next_one[v] = block + next_two[v]

    def sink_two(v, block):
        next_two[v] = block

    @pl.when(jnp.logical_and(step < count, step < count - 2))
    def _():
        amps = amps_of((0, 3))
        first_steps(source, amps, (0, 3), wk, z)
        last_step(amps, (0,), z, sink_zero)

    @pl.when(jnp.logical_and(step < count, step >= count - 2))
    def _():
        amps = amps_of((0,))
        first_steps(source, amps, (0,), wk, z)
        last_step(amps, (0,), z, sink_zero)

    @pl.when(step < count - 1)
    def _():
        amps = amps_of((1, 2))
        first_steps(source, amps, (1, 2), wk, z)
        last_step(amps, (1, 2), z, sink_one)

    @pl.when(step < count - 2)
    def _():
        last_step(amps_of((3,)), (3,), z, sink_two)

    @pl.when(step >= count)
    def _():
        out[...] = jnp.zeros_like(out)


def call(kernel, site, grid, slot_of_step, out_shape, out_spec, accs, flops, scal, lefts, amps, ops):
    def slot_map(rank):
        return lambda i, scal: (slot_of_step(i, scal),) + (0,) * (rank - 1)

    def whole(rank):
        return lambda i, scal: (0,) * rank

    if site == 0:
        left_specs = [pl.BlockSpec((1, W, S, S), slot_map(4))]
    else:
        left_specs = [pl.BlockSpec((1, HALF, S, S), slot_map(4))] * 2 + [pl.BlockSpec((HALF, S, S), whole(3))] * 4
    specs = left_specs + [pl.BlockSpec((1, 4, S, S), slot_map(4))] * 2 + [pl.BlockSpec((6, W, W), whole(3))] * 2
    scratch = [
        pltpu.VMEM((W, S, S) if site else (1, 8, S), BF16),
        pltpu.VMEM((6, 8 * HALF, 8 * W), BF16),
        pltpu.VMEM((4, HALF, S, S), BF16),
    ] + [pltpu.VMEM((HALF, S, S), F32)] * accs
    return pl.pallas_call(
        functools.partial(kernel, site),
        grid_spec=pltpu.PrefetchScalarGridSpec(
            num_scalar_prefetch=1, grid=(grid,), in_specs=specs, out_specs=out_spec, scratch_shapes=scratch
        ),
        out_shape=out_shape,
        cost_estimate=pl.CostEstimate(flops=flops, bytes_accessed=4_000_000, transcendentals=0),
        compiler_params=pltpu.CompilerParams(vmem_limit_bytes=VMEM_LIMIT, dimension_semantics=("arbitrary",)),
    )(scal, *lefts, *amps, *ops)


def last_slot(i, scal):
    return scal[0] - 1


def back_slot(i, scal):
    return jnp.maximum(scal[0] - 1 - i, 0)


def own_slot(i, scal):
    return jnp.minimum(i, scal[0] - 1)


def edge_two(site, *args):
    spec = pl.BlockSpec((HALF, S, S), lambda i, scal: (0, 0, 0))
    shape = jax.ShapeDtypeStruct((HALF, S, S), BF16)
    return call(y_kernel, site, 1, last_slot, shape, spec, 0, 2_000_000_000, *args)


def edge_one(site, *args):
    spec = pl.BlockSpec((HALF, S, S), lambda i, scal: (0, 0, 0))
    shape = jax.ShapeDtypeStruct((HALF, S, S), BF16)
    return call(x_kernel, site, 2, back_slot, shape, spec, 1, 4_000_000_000, *args)


def inner(site, *args):
    spec = pl.BlockSpec((1, HALF, S, S), lambda i, scal: (i, 0, 0, 0))
    shape = jax.ShapeDtypeStruct((4, HALF, S, S), BF16)
    return call(q_kernel, site, 4, own_slot, shape, spec, 2, 12_000_000_000, *args)


def operator_blocks(weight, mask):
    kept = weight.astype(F32) * mask.astype(F32)[:, None, None, :]
    return jnp.stack([kept[:, s, s2, :] for s, s2 in PAIRS]).astype(BF16)


def shards(owners, environment, amplitudes, mpo_weight, mpo_mask, sector_count):
    core = lax.axis_index("site")
    owner = lax.axis_index("sector")
    across = [(c * owners + o, (1 - c) * owners + o) for c in range(2) for o in range(owners)]
    ahead = [(c * owners + o, c * owners + (o + 1) % owners) for c in range(2) for o in range(owners)]

    def swap(x):
        return lax.ppermute(x, AXES, across)

    def onward(x):
        return lax.ppermute(x, AXES, ahead)

    count = lax.dynamic_index_in_dim(sector_count, owner, 0, keepdims=False)
    scal = jnp.stack([count, core, (owner > 0).astype(jnp.int32)]).astype(jnp.int32)
    env = jnp.transpose(environment, (0, 2, 1, 3))
    own_ops = operator_blocks(mpo_weight[0], mpo_mask[0])
    amps = (amplitudes[0], swap(amplitudes[0]))
    ops = (own_ops, swap(own_ops))
    cuts = ((0, 8), (8, HALF))
    pass_on = jnp.logical_and(count == 1, owner > 0)

    lefts = (env,)
    parts = []
    for site in range(2):
        args = (scal, lefts, amps, ops)
        y_out = edge_two(site, *args)
        y_in = [onward(y_out[a:b]) for a, b in cuts]
        x_out = edge_one(site, *args)
        x_in = []
        for (a, b), y in zip(cuts, y_in):
            more = jnp.where(pass_on, y.astype(F32), 0.0)
            x_in.append(onward((x_out[a:b].astype(F32) + more).astype(BF16)))
        inside = inner(site, *args)
        inside_oth = swap(inside)
        y_oth = [swap(y) for y in y_in]
        x_oth = [swap(x) for x in x_in]
        join = lambda xs: jnp.concatenate(xs, axis=0)
        lefts = (inside, inside_oth, join(x_in), join(x_oth), join(y_in), join(y_oth))
        parts.append(lefts)

    def finish(part):
        mine, other, x_own, x_oth, y_own, y_oth = part
        is_in = owner > 0
        halves = []
        for block, x, y in ((mine, x_own, y_own), (other, x_oth, y_oth)):
            zero = block[0].astype(F32) + jnp.where(is_in, x.astype(F32), 0.0)
            one = block[1].astype(F32) + jnp.where(jnp.logical_and(is_in, count > 1), y.astype(F32), 0.0)
            halves.append(jnp.concatenate([jnp.stack([zero, one]).astype(BF16), block[2:]], axis=0))
        return halves

    own_zero, oth_zero = finish(parts[0])
    own_one, oth_one = finish(parts[1])
    first = jnp.where(core == 0, own_zero, oth_one)
    second = jnp.where(core == 0, oth_zero, own_one)
    result = jnp.concatenate([first, second], axis=1)
    return jnp.transpose(result, (0, 2, 1, 3))[None]


def solution(mesh):
    placed = (
        P("sector", None, None, None),
        P("site", "sector", None, None, None),
        P("site", None, None, None, None),
        P("site", None, None),
        P(),
    )
    return jax.shard_map(
        functools.partial(shards, mesh.shape["sector"]),
        mesh=mesh,
        in_specs=placed,
        out_specs=P("site", "sector", None, None, None),
        check_vma=False,
    )
```

```python
import functools

import jax
import jax.numpy as jnp
from jax import lax
from jax.experimental import pallas as pl
from jax.experimental.pallas import tpu as pltpu
from jax.sharding import PartitionSpec as P

S = 128
W = 30
HALF = 15
CUTS = ((0, 8), (8, HALF))
Q_FLOPS = 8_000_000_000
N_CUT = len(CUTS)
AXES = ("site", "sector")
F32 = jnp.float32
BF16 = jnp.bfloat16
MIB = 1024 * 1024
HBM = pl.BlockSpec(memory_space=pltpu.HBM)
VMEM = pl.BlockSpec(memory_space=pltpu.VMEM)
ANY = pl.BlockSpec(memory_space=pl.ANY)


def iota(shape, dim):
    return lax.broadcasted_iota(jnp.int32, shape, dim)


def place(sizes):
    owner = lax.axis_index("sector")
    return sizes[owner], lax.axis_index("site"), owner


def expand_operator(core, site, states, w_own, w_oth, wk):
    row_v = iota((8 * HALF, W), 0) // 8 + core * HALF
    pick_v = (row_v == iota((8 * HALF, W), 1)).astype(BF16)
    spot = iota((W, 8 * W), 1) // 8
    if site:
        spot = jnp.where(core == 0, spot, jnp.where(spot < HALF, spot + HALF, spot - HALF))
    pick_w = (spot == iota((W, 8 * W), 0)).astype(BF16)
    diagonal = (iota((8 * HALF, 8 * W), 0) % 8) == (iota((8 * HALF, 8 * W), 1) % 8)

    def block(s, s2):
        chosen = jnp.where(core == site, w_own[s, s2].astype(F32), w_oth[s, s2].astype(F32)).astype(BF16)
        rows = lax.dot_general(pick_v, chosen, (((1,), (1,)), ((), ())), preferred_element_type=F32).astype(BF16)
        full = jnp.dot(rows, pick_w, preferred_element_type=F32)
        return jnp.where(diagonal, full, 0.0).astype(BF16)

    if 0 in states:
        wk[0, : 8 * HALF, : 8 * W] = block(0, 0)
    if 3 in states:
        wk[1, : 8 * HALF, : 8 * W] = block(3, 3)
    if 1 in states:
        upper = jnp.concatenate([block(1, 1), block(1, 2)], axis=1)
        lower = jnp.concatenate([block(2, 1), block(2, 2)], axis=1)
        wk[2] = jnp.concatenate([upper, lower], axis=0)


def first_steps(left, amps, states, wk, z):
    columns = jnp.concatenate([amps[s] for s in states], axis=1) if len(states) > 1 else amps[states[0]]
    rights = []
    for g in range(8):
        block = left[:, 16 * g : 16 * g + 16, :].reshape(W * 16, S)
        c = jnp.dot(block, columns, preferred_element_type=F32)
        c = c.reshape(W, 16, S * len(states))
        low = c[:, :8, :].reshape(W * 8, S * len(states)).astype(BF16)
        high = c[:, 8:, :].reshape(W * 8, S * len(states)).astype(BF16)
        rights.append(
            {
                s: jnp.concatenate([low[:, S * k : S * k + S], high[:, S * k : S * k + S]], axis=1)
                for k, s in enumerate(states)
            }
        )

    def keep(s, g, total):
        total = total.reshape(HALF, 8, 2 * S)
        z[s, :, 16 * g : 16 * g + 16, :] = jnp.concatenate([total[:, :, :S], total[:, :, S:]], axis=1).astype(BF16)

    for g in range(8):
        for s, p in ((0, 0), (3, 1)):
            if s in states:
                keep(s, g, jnp.dot(wk[p, : 8 * HALF, : 8 * W], rights[g][s], preferred_element_type=F32))
        if 1 in states:
            both = jnp.concatenate([rights[g][1], rights[g][2]], axis=0)
            total = jnp.dot(wk[2], both, preferred_element_type=F32)
            keep(1, g, total[: 8 * HALF])
            keep(2, g, total[8 * HALF :])


def last_step(amps, states, z, sink):
    turned = [amps[s].astype(F32).T.astype(BF16) for s in states]
    lhs = jnp.concatenate(turned, axis=1) if len(states) > 1 else turned[0]

    def right(v):
        return jnp.concatenate([z[s, v] for s in states], axis=0) if len(states) > 1 else z[states[0], v]

    for v in range(0, HALF, 2):
        count = min(2, HALF - v)
        rhs = jnp.concatenate([right(v), right(v + 1)], axis=1) if count > 1 else right(v)
        out = jnp.dot(lhs, rhs, preferred_element_type=F32)
        for i in range(count):
            sink(v + i, out[:, S * i : S * i + S])


def form_left(slot, left, refs):
    @pl.when(slot == 0)
    def _():
        for half in range(2):
            for (a, b), ref in zip(CUTS, refs[0][half]):
                left[half * HALF + a : half * HALF + b] = ref[...]

    for k in (1, 2, 3):
        @pl.when(slot == k)
        def _(k=k):
            for half in range(2):
                left[half * HALF : half * HALF + HALF] = refs[k][half][...]


def grouped(refs):
    rest = refs[2 * N_CUT :]
    return ((refs[:N_CUT], refs[N_CUT : 2 * N_CUT]), *((rest[k], rest[3 + k]) for k in range(3)))


def pick_amp(core, site, amp_refs, slot, s):
    if site:
        return amp_refs[0][slot, s]
    return jnp.where(core == site, amp_refs[0][slot, s].astype(F32), amp_refs[1][slot, s].astype(F32)).astype(BF16)


def y_kernel(site, sizes, lefts, amp_refs, w_own, w_oth, outs, left, wk, z):
    count, core, _ = place(sizes)
    slot = count - 1
    expand_operator(core, site, (3,), w_own, w_oth, wk)
    amps = {3: pick_amp(core, site, amp_refs, slot, 3)}
    if site:
        form_left(slot, left, grouped(lefts))
    first_steps(left if site else lefts[0], amps, (3,), wk, z)

    def sink(v, block):
        for (a, b), out in zip(CUTS, outs):
            if a <= v < b:
                out[v - a] = block.astype(BF16)

    last_step(amps, (3,), z, sink)


def x_kernel(site, sizes, lefts, amp_refs, w_own, w_oth, outs, left, wk, z, acc, *sems):
    count, core, _ = place(sizes)
    prior = jnp.maximum(count - 2, 0)
    if site == 0:
        fetch = pltpu.make_async_copy(lefts[1].at[prior], left, sems[0])
        fetch.start()
    expand_operator(core, site, (1, 2, 3), w_own, w_oth, wk)
    if site:
        form_left(count - 1, left, grouped(lefts))
    amps = {s: pick_amp(core, site, amp_refs, count - 1, s) for s in (1, 2)}
    first_steps(left if site else lefts[0], amps, (1, 2), wk, z)

    def put(read):
        def sink(v, block):
            for (a, b), out in zip(CUTS, outs):
                if a <= v < b:
                    out[v - a] = read(v, block).astype(BF16)

        return sink

    def keep(v, block):
        acc[v] = block

    last_step(amps, (1, 2), z, keep)
    if site == 0:
        fetch.wait()

    @pl.when(count >= 2)
    def _():
        if site:
            form_left(prior, left, grouped(lefts))
        amps = {3: pick_amp(core, site, amp_refs, prior, 3)}
        first_steps(left, amps, (3,), wk, z)
        last_step(amps, (3,), z, put(lambda v, block: acc[v] + block))

    @pl.when(count < 2)
    def _():
        for (a, b), out in zip(CUTS, outs):
            out[...] = acc[a:b].astype(BF16)


def q_kernel(site, sizes, lefts, amp_refs, w_own, w_oth, outs, left, wk, z, next_one, next_two, *sems):
    out = outs[0]
    lefts, y_refs = lefts[:-N_CUT], lefts[-N_CUT:]
    count, core, owner = place(sizes)
    step = pl.program_id(0)

    def fetch(slot):
        return pltpu.make_async_copy(lefts[0].at[slot], left.at[slot % 2], sems[0].at[slot % 2])

    @pl.when(step == 0)
    def _():
        if site == 0:
            fetch(0).start()
        expand_operator(core, site, (0, 1, 2, 3), w_own, w_oth, wk)
        next_one[...] = jnp.zeros_like(next_one)
        next_two[...] = jnp.zeros_like(next_two)

    if site == 0:
        @pl.when(step + 1 < count)
        def _():
            fetch(step + 1).start()

        for s in range(4):
            later_amp = jnp.where(core == 1, amp_refs[0][step, s].astype(F32), amp_refs[1][step, s].astype(F32))
            outs[1][step, s] = later_amp.astype(BF16)

        @pl.when(step < count)
        def _():
            fetch(step).wait()

        source = left.at[step % 2]
    else:
        @pl.when(step < count)
        def _():
            form_left(step, left, grouped(lefts))

        source = left

    @pl.when(jnp.logical_and(step == 1, owner > 0))
    def _():
        for (a, b), ref in zip(CUTS, y_refs):
            next_one[a:b] = next_one[a:b] + ref[...].astype(F32)

    def sink_zero(v, block):
        out[step, v] = (block + next_one[v]).astype(BF16)

    def sink_one(v, block):
        next_one[v] = block + next_two[v]

    def sink_two(v, block):
        next_two[v] = block

    def work(states):
        amps = {s: pick_amp(core, site, amp_refs, step, s) for s in states}
        first_steps(source, amps, states, wk, z)
        last_step(amps, (0,), z, sink_zero)
        if 1 in states:
            last_step(amps, (1, 2), z, sink_one)
        if 3 in states:
            last_step(amps, (3,), z, sink_two)

    @pl.when(step < count - 2)
    def _():
        work((0, 3, 1, 2))

    @pl.when(jnp.logical_and(step == count - 2, step >= 0))
    def _():
        work((0, 1, 2))

    @pl.when(step == count - 1)
    def _():
        work((0,))

    @pl.when(step >= count)
    def _():
        out[step] = jnp.zeros((HALF, S, S), BF16)


CUT_SHAPES = [(b - a, S, S) for a, b in CUTS]


def call(kernel, site, grid, left_specs, shapes, scratch, flops, sizes, lefts, amps, ops, after=()):
    n_left, n_out, n_after, n_amp = len(lefts), len(shapes), len(after), len(amps)

    def body(sizes, *refs):
        left_refs, refs = refs[:n_left], refs[n_left:]
        amp_refs, op_refs, refs = refs[:n_amp], refs[n_amp : n_amp + 2], refs[n_amp + 2 + n_after :]
        kernel(site, sizes, left_refs, amp_refs, *op_refs, refs[:n_out], *refs[n_out:])

    return pl.pallas_call(
        body,
        grid_spec=pltpu.PrefetchScalarGridSpec(
            num_scalar_prefetch=1,
            grid=(grid,),
            in_specs=left_specs + [VMEM] * (n_amp + 2) + [ANY] * n_after,
            out_specs=[VMEM] * n_out,
            scratch_shapes=scratch,
        ),
        out_shape=[jax.ShapeDtypeStruct(shape, BF16) for shape in shapes],
        cost_estimate=pl.CostEstimate(flops=flops, bytes_accessed=4_000_000, transcendentals=0),
        compiler_params=pltpu.CompilerParams(vmem_limit_bytes=24 * MIB, dimension_semantics=("arbitrary",)),
        name=kernel.__name__ + str(site),
    )(sizes, *lefts, *amps, *ops, *after)


def work_space():
    return [pltpu.VMEM((3, 16 * HALF, 16 * W), BF16), pltpu.VMEM((4, HALF, S, S), BF16)]


def edge_two(site, sizes, lefts, amps, ops):
    left = pltpu.VMEM((W, S, S) if site else (1, 8, S), BF16)
    return call(
        y_kernel, site, 1, [VMEM] * len(lefts), CUT_SHAPES, [left] + work_space(), 2_000_000_000, sizes, lefts, amps, ops
    )


def edge_one(site, sizes, lefts, amps, ops, after):
    scratch = [pltpu.VMEM((W, S, S), BF16)] + work_space() + [pltpu.VMEM((HALF, S, S), F32)]
    specs = [VMEM] * len(lefts)
    if site == 0:
        scratch.append(pltpu.SemaphoreType.DMA)
        specs = [VMEM, HBM]
    return call(x_kernel, site, 1, specs, CUT_SHAPES, scratch, 4_000_000_000, sizes, lefts, amps, ops, after)


def inner(site, sizes, lefts, amps, ops, after):
    left = pltpu.VMEM((W, S, S) if site else (2, W, S, S), BF16)
    scratch = [left] + work_space() + [pltpu.VMEM((HALF, S, S), F32)] * 2
    specs, shapes = [VMEM] * len(lefts), [(4, HALF, S, S)]
    if site == 0:
        scratch.append(pltpu.SemaphoreType.DMA((2,)))
        specs, shapes = [HBM] + [VMEM] * N_CUT, shapes + [(4, 4, S, S)]
    return call(q_kernel, site, 4, specs, shapes, scratch, Q_FLOPS, sizes, lefts, amps, ops, after)


def fetch_last(sizes, env):
    def body(sizes, env, out, sem):
        copy = pltpu.make_async_copy(env.at[place(sizes)[0] - 1], out, sem)
        copy.start()
        copy.wait()

    return pl.pallas_call(
        body,
        in_specs=[pl.BlockSpec(memory_space=pltpu.SMEM), HBM],
        out_specs=VMEM,
        scratch_shapes=[pltpu.SemaphoreType.DMA],
        out_shape=jax.ShapeDtypeStruct((W, S, S), BF16),
        compiler_params=pltpu.CompilerParams(vmem_limit_bytes=52 * MIB),
        name="fetch_last",
    )(sizes, env)


def block_copies(site, slots, blocks, out, sems):
    copies = []

    def add(ref, slot, v, length):
        copies.append(pltpu.make_async_copy(ref, out.at[slot, v : v + length], sems.at[len(copies)]))

    for slot in slots:
        for half in range(2):
            which = half if site == 0 else 1 - half
            if slot == 0:
                for (a, b), ref in zip(CUTS, blocks[slot][which]):
                    add(ref, slot, half * HALF + a, b - a)
            else:
                add(blocks[slot][which], slot, half * HALF, HALF)
    for copy in copies:
        copy.start()
    for copy in copies:
        copy.wait()


def finish_early(sizes, first, second):
    n_first, n_in = len(first), len(first) + len(second)

    def body(sizes, *refs):
        one = grouped(refs[:n_first])
        two_refs = refs[n_first:n_in]
        two = (None, *((two_refs[k], two_refs[3 + k]) for k in range(3)))
        out, sems = refs[n_in:]
        core = lax.axis_index("site")

        @pl.when(core == 0)
        def _():
            block_copies(0, range(4), one, out, sems)

        @pl.when(core == 1)
        def _():
            block_copies(1, range(1, 4), two, out, sems)

    return pl.pallas_call(
        body,
        in_specs=[pl.BlockSpec(memory_space=pltpu.SMEM)] + [VMEM] * n_in,
        out_specs=HBM,
        scratch_shapes=[pltpu.SemaphoreType.DMA((2 * N_CUT + 6,))],
        out_shape=jax.ShapeDtypeStruct((4, W, S, S), BF16),
        cost_estimate=pl.CostEstimate(flops=1000, bytes_accessed=1000, transcendentals=0),
        compiler_params=pltpu.CompilerParams(vmem_limit_bytes=4 * MIB),
        name="finish_early",
    )(sizes, *first, *second)


def finish_late(written, own, other):
    def body(written, *refs):
        out, sems = refs[2 * N_CUT :]

        @pl.when(lax.axis_index("site") == 1)
        def _():
            block_copies(1, (0,), ((refs[:N_CUT], refs[N_CUT : 2 * N_CUT]),), out, sems)

    return pl.pallas_call(
        body,
        in_specs=[HBM] + [VMEM] * (2 * N_CUT),
        out_specs=HBM,
        scratch_shapes=[pltpu.SemaphoreType.DMA((2 * N_CUT,))],
        out_shape=jax.ShapeDtypeStruct((4, W, S, S), BF16),
        input_output_aliases={0: 0},
        compiler_params=pltpu.CompilerParams(vmem_limit_bytes=4 * MIB),
        name="finish_late",
    )(written, *own, *other)


def operator_blocks(weight, mask):
    kept = jnp.where(mask[:, None, None, :] != 0, weight, jnp.zeros_like(weight))
    return jnp.transpose(kept, (1, 2, 0, 3))


def later(x, *others):
    return lax.optimization_barrier((x, *others))[0]


def plus(x, y, take):
    return (x.astype(F32) + jnp.where(take, y.astype(F32), 0.0)).astype(BF16)


def shards(owners, environment, amplitudes, mpo_weight, mpo_mask, sector_count):
    owner = lax.axis_index("sector")
    across = [(c * owners + o, (1 - c) * owners + o) for c in range(2) for o in range(owners)]
    ahead = [(c * owners + o, c * owners + (o + 1) % owners) for c in range(2) for o in range(owners)]

    def swap(x):
        return lax.ppermute(x, AXES, across)

    def onward(x):
        return lax.ppermute(x, AXES, ahead)

    env = jnp.transpose(environment, (0, 2, 1, 3))
    own_ops = operator_blocks(mpo_weight[0], mpo_mask[0])
    amps = (amplitudes[0], swap(amplitudes[0]))
    ops = (own_ops, swap(own_ops))

    env_last = fetch_last(sector_count, env)
    edge_left, back_left, lefts = (env_last,), (env_last, env), (env,)
    inward = owner > 0
    for site in range(2):
        y_out = edge_two(site, sector_count, edge_left, amps, ops)
        y_in = [onward(y) for y in y_out]
        if site == 0:
            count = lax.dynamic_index_in_dim(later(sector_count, y_out[0]), owner, 0, keepdims=False)
            pass_on = jnp.logical_and(count == 1, inward)
        x_out = edge_one(site, sector_count, back_left, amps, ops, y_out)
        x_sent = [plus(x, y, pass_on) for x, y in zip(x_out, y_in)]
        x_in = [onward(x) for x in x_sent]
        made = inner(site, sector_count, (*lefts, *y_in), amps, ops, x_sent)
        inside = made[0]
        rest = [inside[k] for k in (1, 2, 3)]
        rest_oth = [swap(later(part, y_in[-1])) for part in rest]
        zero = [plus(later(inside, x)[0, a:b], x, inward) for (a, b), x in zip(CUTS, x_in)]
        if site == 0:
            zero_oth = [swap(block) for block in zero]
            lefts = edge_left = back_left = first = (*zero, *zero_oth, *rest, *rest_oth)
            amps = (made[1],)
        else:
            written = finish_early(sector_count, first, (*rest, *rest_oth))
            zero_oth = [swap(block) for block in zero]
            result = finish_late(written, zero, zero_oth)
    return jnp.transpose(result, (0, 2, 1, 3))[None]


def solution(mesh):
    placed = (
        P("sector", None, None, None),
        P("site", "sector", None, None, None),
        P("site", None, None, None, None),
        P("site", None, None),
        P(),
    )
    return jax.shard_map(
        functools.partial(shards, mesh.shape["sector"]),
        mesh=mesh,
        in_specs=placed,
        out_specs=P("site", "sector", None, None, None),
        check_vma=False,
    )
```

```python
import functools

import jax
import jax.numpy as jnp
from jax import lax
from jax.experimental import pallas as pl
from jax.experimental.pallas import tpu as pltpu
from jax.sharding import PartitionSpec as P

S = 128
W = 30
HALF = 15
CUTS = ((0, 8), (8, HALF))
Q_FLOPS = 8_000_000_000
OPEN = 0
N_CUT = len(CUTS)
AXES = ("site", "sector")
F32 = jnp.float32
BF16 = jnp.bfloat16
MIB = 1024 * 1024
HBM = pl.BlockSpec(memory_space=pltpu.HBM)
VMEM = pl.BlockSpec(memory_space=pltpu.VMEM)
ANY = pl.BlockSpec(memory_space=pl.ANY)


def iota(shape, dim):
    return lax.broadcasted_iota(jnp.int32, shape, dim)


def place(sizes):
    owner = lax.axis_index("sector")
    return sizes[owner], lax.axis_index("site"), owner


def expand_operator(core, site, states, w_own, w_oth, wk):
    row_v = iota((8 * HALF, W), 0) // 8 + core * HALF
    pick_v = (row_v == iota((8 * HALF, W), 1)).astype(BF16)
    spot = iota((W, 8 * W), 1) // 8
    if site:
        spot = jnp.where(core == 0, spot, jnp.where(spot < HALF, spot + HALF, spot - HALF))
    pick_w = (spot == iota((W, 8 * W), 0)).astype(BF16)
    diagonal = (iota((8 * HALF, 8 * W), 0) % 8) == (iota((8 * HALF, 8 * W), 1) % 8)

    def block(s, s2):
        chosen = jnp.where(core == site, w_own[s, s2].astype(F32), w_oth[s, s2].astype(F32)).astype(BF16)
        rows = lax.dot_general(pick_v, chosen, (((1,), (1,)), ((), ())), preferred_element_type=F32).astype(BF16)
        full = jnp.dot(rows, pick_w, preferred_element_type=F32)
        return jnp.where(diagonal, full, 0.0).astype(BF16)

    if 0 in states:
        wk[0, : 8 * HALF, : 8 * W] = block(0, 0)
    if 3 in states:
        wk[1, : 8 * HALF, : 8 * W] = block(3, 3)
    if 1 in states:
        upper = jnp.concatenate([block(1, 1), block(1, 2)], axis=1)
        lower = jnp.concatenate([block(2, 1), block(2, 2)], axis=1)
        wk[2] = jnp.concatenate([upper, lower], axis=0)


def first_steps(left, amps, states, wk, z):
    columns = jnp.concatenate([amps[s] for s in states], axis=1) if len(states) > 1 else amps[states[0]]
    rights = []
    for g in range(8):
        block = left[:, 16 * g : 16 * g + 16, :].reshape(W * 16, S)
        c = jnp.dot(block, columns, preferred_element_type=F32)
        c = c.reshape(W, 16, S * len(states))
        low = c[:, :8, :].reshape(W * 8, S * len(states)).astype(BF16)
        high = c[:, 8:, :].reshape(W * 8, S * len(states)).astype(BF16)
        rights.append(
            {
                s: jnp.concatenate([low[:, S * k : S * k + S], high[:, S * k : S * k + S]], axis=1)
                for k, s in enumerate(states)
            }
        )

    def keep(s, g, total):
        total = total.reshape(HALF, 8, 2 * S)
        z[s, :, 16 * g : 16 * g + 16, :] = jnp.concatenate([total[:, :, :S], total[:, :, S:]], axis=1).astype(BF16)

    for g in range(8):
        for s, p in ((0, 0), (3, 1)):
            if s in states:
                keep(s, g, jnp.dot(wk[p, : 8 * HALF, : 8 * W], rights[g][s], preferred_element_type=F32))
        if 1 in states:
            both = jnp.concatenate([rights[g][1], rights[g][2]], axis=0)
            total = jnp.dot(wk[2], both, preferred_element_type=F32)
            keep(1, g, total[: 8 * HALF])
            keep(2, g, total[8 * HALF :])


def last_step(amps, states, z, sink):
    turned = [amps[s].astype(F32).T.astype(BF16) for s in states]
    lhs = jnp.concatenate(turned, axis=1) if len(states) > 1 else turned[0]

    def right(v):
        return jnp.concatenate([z[s, v] for s in states], axis=0) if len(states) > 1 else z[states[0], v]

    for v in range(0, HALF, 2):
        count = min(2, HALF - v)
        rhs = jnp.concatenate([right(v), right(v + 1)], axis=1) if count > 1 else right(v)
        out = jnp.dot(lhs, rhs, preferred_element_type=F32)
        for i in range(count):
            sink(v + i, out[:, S * i : S * i + S])


def form_left(slot, left, refs):
    @pl.when(slot == 0)
    def _():
        for half in range(2):
            for (a, b), ref in zip(CUTS, refs[0][half]):
                left[half * HALF + a : half * HALF + b] = ref[...]

    for k in (1, 2, 3):
        @pl.when(slot == k)
        def _(k=k):
            for half in range(2):
                left[half * HALF : half * HALF + HALF] = refs[k][half][...]


def grouped(refs):
    rest = refs[2 * N_CUT :]
    return ((refs[:N_CUT], refs[N_CUT : 2 * N_CUT]), *((rest[k], rest[3 + k]) for k in range(3)))


def pick_amp(core, site, amp_refs, slot, s):
    if site:
        return amp_refs[0][slot, s]
    return jnp.where(core == site, amp_refs[0][slot, s].astype(F32), amp_refs[1][slot, s].astype(F32)).astype(BF16)


def y_kernel(site, sizes, lefts, amp_refs, w_own, w_oth, outs, left, wk, z):
    count, core, _ = place(sizes)
    slot = count - 1
    expand_operator(core, site, (3,), w_own, w_oth, wk)
    amps = {3: pick_amp(core, site, amp_refs, slot, 3)}
    if site:
        form_left(slot, left, grouped(lefts))
    first_steps(left if site else lefts[0], amps, (3,), wk, z)

    def sink(v, block):
        for (a, b), out in zip(CUTS, outs):
            if a <= v < b:
                out[v - a] = block.astype(BF16)

    last_step(amps, (3,), z, sink)


def x_kernel(site, sizes, lefts, amp_refs, w_own, w_oth, outs, left, wk, z, acc, *sems):
    count, core, _ = place(sizes)
    prior = jnp.maximum(count - 2, 0)
    if site == 0:
        fetch = pltpu.make_async_copy(lefts[1].at[prior], left, sems[0])
        fetch.start()
    expand_operator(core, site, (1, 2, 3), w_own, w_oth, wk)
    if site:
        form_left(count - 1, left, grouped(lefts))
    amps = {s: pick_amp(core, site, amp_refs, count - 1, s) for s in (1, 2)}
    first_steps(left if site else lefts[0], amps, (1, 2), wk, z)

    def put(read):
        def sink(v, block):
            for (a, b), out in zip(CUTS, outs):
                if a <= v < b:
                    out[v - a] = read(v, block).astype(BF16)

        return sink

    def keep(v, block):
        acc[v] = block

    last_step(amps, (1, 2), z, keep)
    if site == 0:
        fetch.wait()

    @pl.when(count >= 2)
    def _():
        if site:
            form_left(prior, left, grouped(lefts))
        amps = {3: pick_amp(core, site, amp_refs, prior, 3)}
        first_steps(left, amps, (3,), wk, z)
        last_step(amps, (3,), z, put(lambda v, block: acc[v] + block))

    @pl.when(count < 2)
    def _():
        for (a, b), out in zip(CUTS, outs):
            out[...] = acc[a:b].astype(BF16)


def q_kernel(site, sizes, lefts, amp_refs, w_own, w_oth, outs, left, wk, z, next_one, next_two, *sems):
    out = outs[0]
    lefts, y_refs = lefts[:-N_CUT], lefts[-N_CUT:]
    count, core, owner = place(sizes)
    step = pl.program_id(0)

    def fetch(slot):
        return pltpu.make_async_copy(lefts[0].at[slot], left.at[slot % 2], sems[0].at[slot % 2])

    @pl.when(step == 0)
    def _():
        if site == 0:
            fetch(0).start()
        else:
            pl.when(core == 0)(lambda: start_all(known_blocks(lefts, outs[1], sems[0])))
        expand_operator(core, site, (0, 1, 2, 3), w_own, w_oth, wk)
        next_one[...] = jnp.zeros_like(next_one)
        next_two[...] = jnp.zeros_like(next_two)

    if site == 0:
        @pl.when(step + 1 < count)
        def _():
            fetch(step + 1).start()

        for s in range(4):
            later_amp = jnp.where(core == 1, amp_refs[0][step, s].astype(F32), amp_refs[1][step, s].astype(F32))
            outs[1][step, s] = later_amp.astype(BF16)

        @pl.when(step < count)
        def _():
            fetch(step).wait()

        source = left.at[step % 2]
    else:
        @pl.when(step < count)
        def _():
            form_left(step, left, grouped(lefts))

        source = left

    @pl.when(jnp.logical_and(step == 1, owner > 0))
    def _():
        for (a, b), ref in zip(CUTS, y_refs):
            next_one[a:b] = next_one[a:b] + ref[...].astype(F32)

    def sink_zero(v, block):
        out[step, v] = (block + next_one[v]).astype(BF16)

    def sink_one(v, block):
        next_one[v] = block + next_two[v]

    def sink_two(v, block):
        next_two[v] = block

    def work(states):
        amps = {s: pick_amp(core, site, amp_refs, step, s) for s in states}
        first_steps(source, amps, states, wk, z)
        last_step(amps, (0,), z, sink_zero)
        if 1 in states:
            last_step(amps, (1, 2), z, sink_one)
        if 3 in states:
            last_step(amps, (3,), z, sink_two)

    @pl.when(step < count - 2)
    def _():
        work((0, 3, 1, 2))

    @pl.when(jnp.logical_and(step == count - 2, step >= 0))
    def _():
        work((0, 1, 2))

    @pl.when(step == count - 1)
    def _():
        work((0,))

    @pl.when(step >= count)
    def _():
        out[step] = jnp.zeros((HALF, S, S), BF16)

    if site:
        def own_half():
            return [pltpu.make_async_copy(out.at[k], outs[1].at[k, HALF:], sems[0].at[k - 1]) for k in (1, 2, 3)]

        @pl.when(step == 3)
        def _():
            pl.when(core == 0)(lambda: wait_all(known_blocks(lefts, outs[1], sems[0])))

            @pl.when(core == 1)
            def _():
                start_all(own_half())
                wait_all(own_half())


def start_all(copies):
    for copy in copies:
        copy.start()


def wait_all(copies):
    for copy in copies:
        copy.wait()


def known_blocks(lefts, out, sems):
    copies = []

    def add(ref, slot, v, length):
        copies.append(pltpu.make_async_copy(ref, out.at[slot, v : v + length], sems.at[len(copies)]))

    blocks = grouped(lefts)
    for half in range(2):
        for (a, b), ref in zip(CUTS, blocks[0][half]):
            add(ref, 0, half * HALF + a, b - a)
        for slot in (1, 2, 3):
            add(blocks[slot][half], slot, half * HALF, HALF)
    return copies


CUT_SHAPES = [(b - a, S, S) for a, b in CUTS]


def call(kernel, site, grid, left_specs, shapes, scratch, flops, sizes, lefts, amps, ops, after=(), out_specs=None):
    n_left, n_out, n_after, n_amp = len(lefts), len(shapes), len(after), len(amps)

    def body(sizes, *refs):
        left_refs, refs = refs[:n_left], refs[n_left:]
        amp_refs, op_refs, refs = refs[:n_amp], refs[n_amp : n_amp + 2], refs[n_amp + 2 + n_after :]
        kernel(site, sizes, left_refs, amp_refs, *op_refs, refs[:n_out], *refs[n_out:])

    return pl.pallas_call(
        body,
        grid_spec=pltpu.PrefetchScalarGridSpec(
            num_scalar_prefetch=1,
            grid=(grid,),
            in_specs=left_specs + [VMEM] * (n_amp + 2) + [ANY] * n_after,
            out_specs=out_specs or [VMEM] * n_out,
            scratch_shapes=scratch,
        ),
        out_shape=[jax.ShapeDtypeStruct(shape, BF16) for shape in shapes],
        cost_estimate=pl.CostEstimate(flops=flops, bytes_accessed=4_000_000, transcendentals=0),
        compiler_params=pltpu.CompilerParams(vmem_limit_bytes=(46 if kernel is q_kernel and site == 0 else 24) * MIB, dimension_semantics=("arbitrary",)),
        name=kernel.__name__ + str(site),
    )(sizes, *lefts, *amps, *ops, *after)


def work_space():
    return [pltpu.VMEM((3, 16 * HALF, 16 * W), BF16), pltpu.VMEM((4, HALF, S, S), BF16)]


def edge_two(site, sizes, lefts, amps, ops):
    left = pltpu.VMEM((W, S, S) if site else (1, 8, S), BF16)
    return call(
        y_kernel, site, 1, [VMEM] * len(lefts), CUT_SHAPES, [left] + work_space(), 2_000_000_000, sizes, lefts, amps, ops
    )


def edge_one(site, sizes, lefts, amps, ops, after):
    scratch = [pltpu.VMEM((W, S, S), BF16)] + work_space() + [pltpu.VMEM((HALF, S, S), F32)]
    specs = [VMEM] * len(lefts)
    if site == 0:
        scratch.append(pltpu.SemaphoreType.DMA)
        specs = [VMEM, HBM]
    return call(x_kernel, site, 1, specs, CUT_SHAPES, scratch, 4_000_000_000, sizes, lefts, amps, ops, after)


def inner(site, sizes, lefts, amps, ops, after):
    left = pltpu.VMEM((W, S, S) if site else (2, W, S, S), BF16)
    scratch = [left] + work_space() + [pltpu.VMEM((HALF, S, S), F32)] * 2
    specs, shapes = [VMEM] * len(lefts), [(4, HALF, S, S), (4, W, S, S) if site else (4, 4, S, S)]
    scratch.append(pltpu.SemaphoreType.DMA((2 * N_CUT + 6 if site else 2,)))
    if site == 0:
        specs = [HBM] + [VMEM] * N_CUT
    out_specs = [VMEM, HBM if site else VMEM]
    return call(q_kernel, site, 4, specs, shapes, scratch, Q_FLOPS, sizes, lefts, amps, ops, after, out_specs)


def fetch_last(sizes, env):
    def body(sizes, env, out, sem):
        copy = pltpu.make_async_copy(env.at[place(sizes)[0] - 1], out, sem)
        copy.start()
        copy.wait()

    return pl.pallas_call(
        body,
        in_specs=[pl.BlockSpec(memory_space=pltpu.SMEM), HBM],
        out_specs=VMEM,
        scratch_shapes=[pltpu.SemaphoreType.DMA],
        out_shape=jax.ShapeDtypeStruct((W, S, S), BF16),
        compiler_params=pltpu.CompilerParams(vmem_limit_bytes=52 * MIB),
        name="fetch_last",
    )(sizes, env)


def finish(written, zero, zero_oth, rest_oth):
    def body(written, *refs):
        own, other, rest = refs[:N_CUT], refs[N_CUT : 2 * N_CUT], refs[2 * N_CUT : 2 * N_CUT + 3]
        out, sems = refs[2 * N_CUT + 3 :]

        @pl.when(lax.axis_index("site") == 1)
        def _():
            copies = []

            def add(ref, slot, v, length):
                copies.append(pltpu.make_async_copy(ref, out.at[slot, v : v + length], sems.at[len(copies)]))

            for k in range(3):
                add(rest[k], k + 1, 0, HALF)
            for half, parts in enumerate((other, own)):
                for (a, b), ref in zip(CUTS, parts):
                    add(ref, 0, half * HALF + a, b - a)
            start_all(copies)
            wait_all(copies)

    return pl.pallas_call(
        body,
        in_specs=[HBM] + [VMEM] * (2 * N_CUT + 3),
        out_specs=HBM,
        scratch_shapes=[pltpu.SemaphoreType.DMA((2 * N_CUT + 3,))],
        out_shape=jax.ShapeDtypeStruct((4, W, S, S), BF16),
        input_output_aliases={0: 0},
        compiler_params=pltpu.CompilerParams(vmem_limit_bytes=4 * MIB),
        name="finish",
    )(written, *zero, *zero_oth, *rest_oth)


def operator_blocks(weight, mask):
    kept = jnp.where(mask[:, None, None, :] != 0, weight, jnp.zeros_like(weight))
    return jnp.transpose(kept, (1, 2, 0, 3))


def later(x, *others):
    return lax.optimization_barrier((x, *others))[0]


def plus(x, y, take):
    return (x.astype(F32) + jnp.where(take, y.astype(F32), 0.0)).astype(BF16)


def shards(owners, environment, amplitudes, mpo_weight, mpo_mask, sector_count):
    owner = lax.axis_index("sector")
    across = [(c * owners + o, (1 - c) * owners + o) for c in range(2) for o in range(owners)]
    ahead = [(c * owners + o, c * owners + (o + 1) % owners) for c in range(2) for o in range(owners)]

    def swap(x):
        return lax.ppermute(x, AXES, across)

    def onward(x):
        return lax.ppermute(x, AXES, ahead)

    def final_onward(x):
        return lax.ppermute(x, AXES, [pair for pair in ahead if pair[1] % owners > 0])

    env = jnp.transpose(environment, (0, 2, 1, 3))
    own_ops = operator_blocks(mpo_weight[0], mpo_mask[0])
    amps = (amplitudes[0], swap(amplitudes[0]))
    ops = (own_ops, swap(own_ops))

    env_last = fetch_last(sector_count, env)
    edge_left, back_left, lefts = (env_last,), (env_last, env), (env,)
    inward = owner > 0
    for site in range(2):
        y_out = edge_two(site, sector_count, edge_left, amps, ops)
        y_in = [onward(y) for y in y_out]
        if site == 0:
            count = lax.dynamic_index_in_dim(later(sector_count, y_out[0]), owner, 0, keepdims=False)
            pass_on = jnp.logical_and(count == 1, inward)
        x_out = edge_one(site, sector_count, back_left, amps, ops, y_out)
        x_sent = [plus(x, y, pass_on) for x, y in zip(x_out, y_in)]
        x_in = [(final_onward if k == OPEN else onward)(x) for k, x in enumerate(x_sent)]
        made = inner(site, sector_count, (*lefts, *y_in), amps, ops, x_sent)
        inside = made[0]
        rest = [inside[k] for k in (1, 2, 3)]
        rest_oth = [swap(later(part, y_in[-1])) for part in rest]
        zero = [plus(later(inside, x)[0, a:b], x, inward) for (a, b), x in zip(CUTS, x_in)]
        if site == 0:
            zero_oth = [swap(block) for block in zero]
            lefts = edge_left = back_left = (*zero, *zero_oth, *rest, *rest_oth)
            amps = (made[1],)
        else:
            zero_oth = [swap(block) for block in zero]
            result = finish(made[1], zero, zero_oth, rest_oth)
    return jnp.transpose(result, (0, 2, 1, 3))[None]


def solution(mesh):
    placed = (
        P("sector", None, None, None),
        P("site", "sector", None, None, None),
        P("site", None, None, None, None),
        P("site", None, None),
        P(),
    )
    return jax.shard_map(
        functools.partial(shards, mesh.shape["sector"]),
        mesh=mesh,
        in_specs=placed,
        out_specs=P("site", "sector", None, None, None),
        check_vma=False,
    )
```

```python
import functools

import jax
import jax.numpy as jnp
from jax import lax
from jax.experimental import pallas as pl
from jax.experimental.pallas import tpu as pltpu
from jax.sharding import PartitionSpec as P

S = 128
W = 30
HALF = 15
CUTS = ((0, 8), (8, HALF))
Q_FLOPS = 8_000_000_000
OPEN = 0
N_CUT = len(CUTS)
AXES = ("site", "sector")
F32 = jnp.float32
BF16 = jnp.bfloat16
MIB = 1024 * 1024
HBM = pl.BlockSpec(memory_space=pltpu.HBM)
VMEM = pl.BlockSpec(memory_space=pltpu.VMEM)
ANY = pl.BlockSpec(memory_space=pl.ANY)


def iota(shape, dim):
    return lax.broadcasted_iota(jnp.int32, shape, dim)


def place(sizes):
    owner = lax.axis_index("sector")
    return sizes[owner], lax.axis_index("site"), owner


def expand_operator(core, site, states, w_own, w_oth, wk):
    row_v = iota((8 * HALF, W), 0) // 8 + core * HALF
    pick_v = (row_v == iota((8 * HALF, W), 1)).astype(BF16)
    spot = iota((W, 8 * W), 1) // 8
    if site:
        spot = jnp.where(core == 0, spot, jnp.where(spot < HALF, spot + HALF, spot - HALF))
    pick_w = (spot == iota((W, 8 * W), 0)).astype(BF16)
    diagonal = (iota((8 * HALF, 8 * W), 0) % 8) == (iota((8 * HALF, 8 * W), 1) % 8)

    def block(s, s2):
        chosen = jnp.where(core == site, w_own[s, s2].astype(F32), w_oth[s, s2].astype(F32)).astype(BF16)
        rows = lax.dot_general(pick_v, chosen, (((1,), (1,)), ((), ())), preferred_element_type=F32).astype(BF16)
        full = jnp.dot(rows, pick_w, preferred_element_type=F32)
        return jnp.where(diagonal, full, 0.0).astype(BF16)

    if 0 in states:
        wk[0, : 8 * HALF, : 8 * W] = block(0, 0)
    if 3 in states:
        wk[1, : 8 * HALF, : 8 * W] = block(3, 3)
    if 1 in states:
        upper = jnp.concatenate([block(1, 1), block(1, 2)], axis=1)
        lower = jnp.concatenate([block(2, 1), block(2, 2)], axis=1)
        wk[2] = jnp.concatenate([upper, lower], axis=0)


def first_steps(left, amps, states, wk, z):
    columns = jnp.concatenate([amps[s] for s in states], axis=1) if len(states) > 1 else amps[states[0]]
    rights = []
    for g in range(8):
        block = left[:, 16 * g : 16 * g + 16, :].reshape(W * 16, S)
        c = jnp.dot(block, columns, preferred_element_type=F32)
        c = c.reshape(W, 16, S * len(states))
        low = c[:, :8, :].reshape(W * 8, S * len(states)).astype(BF16)
        high = c[:, 8:, :].reshape(W * 8, S * len(states)).astype(BF16)
        rights.append(
            {
                s: jnp.concatenate([low[:, S * k : S * k + S], high[:, S * k : S * k + S]], axis=1)
                for k, s in enumerate(states)
            }
        )

    def keep(s, g, total):
        total = total.reshape(HALF, 8, 2 * S)
        z[s, :, 16 * g : 16 * g + 16, :] = jnp.concatenate([total[:, :, :S], total[:, :, S:]], axis=1).astype(BF16)

    for g in range(8):
        for s, p in ((0, 0), (3, 1)):
            if s in states:
                keep(s, g, jnp.dot(wk[p, : 8 * HALF, : 8 * W], rights[g][s], preferred_element_type=F32))
        if 1 in states:
            both = jnp.concatenate([rights[g][1], rights[g][2]], axis=0)
            total = jnp.dot(wk[2], both, preferred_element_type=F32)
            keep(1, g, total[: 8 * HALF])
            keep(2, g, total[8 * HALF :])


def last_step(amps, states, z, sink):
    turned = [amps[s].astype(F32).T.astype(BF16) for s in states]
    lhs = jnp.concatenate(turned, axis=1) if len(states) > 1 else turned[0]

    def right(v):
        return jnp.concatenate([z[s, v] for s in states], axis=0) if len(states) > 1 else z[states[0], v]

    for v in range(0, HALF, 2):
        count = min(2, HALF - v)
        rhs = jnp.concatenate([right(v), right(v + 1)], axis=1) if count > 1 else right(v)
        out = jnp.dot(lhs, rhs, preferred_element_type=F32)
        for i in range(count):
            sink(v + i, out[:, S * i : S * i + S])


def form_left(slot, left, refs):
    @pl.when(slot == 0)
    def _():
        for half in range(2):
            for (a, b), ref in zip(CUTS, refs[0][half]):
                left[half * HALF + a : half * HALF + b] = ref[...]

    for k in (1, 2, 3):
        @pl.when(slot == k)
        def _(k=k):
            for half in range(2):
                left[half * HALF : half * HALF + HALF] = refs[k][half][...]


def grouped(refs):
    rest = refs[2 * N_CUT :]
    return ((refs[:N_CUT], refs[N_CUT : 2 * N_CUT]), *((rest[k], rest[3 + k]) for k in range(3)))


def pick_amp(core, site, amp_refs, slot, s):
    if site:
        return amp_refs[0][slot, s]
    return jnp.where(core == site, amp_refs[0][slot, s].astype(F32), amp_refs[1][slot, s].astype(F32)).astype(BF16)


def y_kernel(site, sizes, lefts, amp_refs, w_own, w_oth, outs, left, wk, z):
    count, core, _ = place(sizes)
    slot = count - 1
    expand_operator(core, site, (3,), w_own, w_oth, wk)
    amps = {3: pick_amp(core, site, amp_refs, slot, 3)}
    if site:
        form_left(slot, left, grouped(lefts))
    first_steps(left if site else lefts[0], amps, (3,), wk, z)

    def sink(v, block):
        for (a, b), out in zip(CUTS, outs):
            if a <= v < b:
                out[v - a] = block.astype(BF16)

    last_step(amps, (3,), z, sink)


def x_kernel(site, sizes, lefts, amp_refs, w_own, w_oth, outs, left, wk, z, acc, *sems):
    count, core, _ = place(sizes)
    prior = jnp.maximum(count - 2, 0)
    if site == 0:
        fetch = pltpu.make_async_copy(lefts[1].at[prior], left, sems[0])
        fetch.start()
    expand_operator(core, site, (1, 2, 3), w_own, w_oth, wk)
    if site:
        form_left(count - 1, left, grouped(lefts))
    amps = {s: pick_amp(core, site, amp_refs, count - 1, s) for s in (1, 2)}
    first_steps(left if site else lefts[0], amps, (1, 2), wk, z)

    def put(read):
        def sink(v, block):
            for (a, b), out in zip(CUTS, outs):
                if a <= v < b:
                    out[v - a] = read(v, block).astype(BF16)

        return sink

    def keep(v, block):
        acc[v] = block

    last_step(amps, (1, 2), z, keep)
    if site == 0:
        fetch.wait()

    @pl.when(count >= 2)
    def _():
        if site:
            form_left(prior, left, grouped(lefts))
        amps = {3: pick_amp(core, site, amp_refs, prior, 3)}
        first_steps(left, amps, (3,), wk, z)
        last_step(amps, (3,), z, put(lambda v, block: acc[v] + block))

    @pl.when(count < 2)
    def _():
        for (a, b), out in zip(CUTS, outs):
            out[...] = acc[a:b].astype(BF16)


def q_kernel(site, sizes, lefts, amp_refs, w_own, w_oth, outs, left, wk, z, next_one, next_two, *sems):
    out = outs[0]
    lefts, y_refs = lefts[:-N_CUT], lefts[-N_CUT:]
    count, core, owner = place(sizes)
    step = pl.program_id(0)

    def fetch(slot):
        return pltpu.make_async_copy(lefts[0].at[slot], left.at[slot % 2], sems[0].at[slot % 2])

    @pl.when(step == 0)
    def _():
        if site == 0:
            fetch(0).start()
        else:
            pl.when(core == 0)(lambda: start_all(known_blocks(lefts, outs[1], sems[0])))
        expand_operator(core, site, (0, 1, 2, 3), w_own, w_oth, wk)
        next_one[...] = jnp.zeros_like(next_one)
        next_two[...] = jnp.zeros_like(next_two)

    if site == 0:
        @pl.when(step + 1 < count)
        def _():
            fetch(step + 1).start()

        for s in range(4):
            later_amp = jnp.where(core == 1, amp_refs[0][step, s].astype(F32), amp_refs[1][step, s].astype(F32))
            outs[1][step, s] = later_amp.astype(BF16)

        @pl.when(step < count)
        def _():
            fetch(step).wait()

        source = left.at[step % 2]
    else:
        @pl.when(step < count)
        def _():
            form_left(step, left, grouped(lefts))

        source = left

    @pl.when(jnp.logical_and(step == 1, owner > 0))
    def _():
        for (a, b), ref in zip(CUTS, y_refs):
            next_one[a:b] = next_one[a:b] + ref[...].astype(F32)

    def sink_zero(v, block):
        out[step, v] = (block + next_one[v]).astype(BF16)

    def sink_one(v, block):
        next_one[v] = block + next_two[v]

    def sink_two(v, block):
        next_two[v] = block

    def work(states):
        amps = {s: pick_amp(core, site, amp_refs, step, s) for s in states}
        first_steps(source, amps, states, wk, z)
        last_step(amps, (0,), z, sink_zero)
        if 1 in states:
            last_step(amps, (1, 2), z, sink_one)
        if 3 in states:
            last_step(amps, (3,), z, sink_two)

    @pl.when(step < count - 2)
    def _():
        work((0, 3, 1, 2))

    @pl.when(jnp.logical_and(step == count - 2, step >= 0))
    def _():
        work((0, 1, 2))

    @pl.when(step == count - 1)
    def _():
        work((0,))

    @pl.when(step >= count)
    def _():
        out[step] = jnp.zeros((HALF, S, S), BF16)

    if site:
        def own_half():
            return [pltpu.make_async_copy(out.at[k], outs[1].at[k, HALF:], sems[0].at[k - 1]) for k in (1, 2, 3)]

        @pl.when(step == 3)
        def _():
            pl.when(core == 0)(lambda: wait_all(known_blocks(lefts, outs[1], sems[0])))

            @pl.when(core == 1)
            def _():
                start_all(own_half())
                wait_all(own_half())


def start_all(copies):
    for copy in copies:
        copy.start()


def wait_all(copies):
    for copy in copies:
        copy.wait()


def known_blocks(lefts, out, sems):
    copies = []

    def add(ref, slot, v, length):
        copies.append(pltpu.make_async_copy(ref, out.at[slot, v : v + length], sems.at[len(copies)]))

    blocks = grouped(lefts)
    for half in range(2):
        for (a, b), ref in zip(CUTS, blocks[0][half]):
            add(ref, 0, half * HALF + a, b - a)
        for slot in (1, 2, 3):
            add(blocks[slot][half], slot, half * HALF, HALF)
    return copies


CUT_SHAPES = [(b - a, S, S) for a, b in CUTS]


def call(kernel, site, grid, left_specs, shapes, scratch, flops, sizes, lefts, amps, ops, after=(), out_specs=None):
    n_left, n_out, n_after, n_amp = len(lefts), len(shapes), len(after), len(amps)

    def body(sizes, *refs):
        left_refs, refs = refs[:n_left], refs[n_left:]
        amp_refs, op_refs, refs = refs[:n_amp], refs[n_amp : n_amp + 2], refs[n_amp + 2 + n_after :]
        kernel(site, sizes, left_refs, amp_refs, *op_refs, refs[:n_out], *refs[n_out:])

    return pl.pallas_call(
        body,
        grid_spec=pltpu.PrefetchScalarGridSpec(
            num_scalar_prefetch=1,
            grid=(grid,),
            in_specs=left_specs + [VMEM] * (n_amp + 2) + [ANY] * n_after,
            out_specs=out_specs or [VMEM] * n_out,
            scratch_shapes=scratch,
        ),
        out_shape=[jax.ShapeDtypeStruct(shape, BF16) for shape in shapes],
        cost_estimate=pl.CostEstimate(flops=flops, bytes_accessed=4_000_000, transcendentals=0),
        compiler_params=pltpu.CompilerParams(vmem_limit_bytes=(46 if kernel is q_kernel and site == 0 else 24) * MIB, dimension_semantics=("arbitrary",)),
        name=kernel.__name__ + str(site),
    )(sizes, *lefts, *amps, *ops, *after)


def work_space():
    return [pltpu.VMEM((3, 16 * HALF, 16 * W), BF16), pltpu.VMEM((4, HALF, S, S), BF16)]


def edge_two(site, sizes, lefts, amps, ops):
    left = pltpu.VMEM((W, S, S) if site else (1, 8, S), BF16)
    return call(
        y_kernel, site, 1, [VMEM] * len(lefts), CUT_SHAPES, [left] + work_space(), 2_000_000_000, sizes, lefts, amps, ops
    )


def edge_one(site, sizes, lefts, amps, ops, after):
    scratch = [pltpu.VMEM((W, S, S), BF16)] + work_space() + [pltpu.VMEM((HALF, S, S), F32)]
    specs = [VMEM] * len(lefts)
    if site == 0:
        scratch.append(pltpu.SemaphoreType.DMA)
        specs = [VMEM, HBM]
    return call(x_kernel, site, 1, specs, CUT_SHAPES, scratch, 4_000_000_000, sizes, lefts, amps, ops, after)


def inner(site, sizes, lefts, amps, ops, after):
    left = pltpu.VMEM((W, S, S) if site else (2, W, S, S), BF16)
    scratch = [left] + work_space() + [pltpu.VMEM((HALF, S, S), F32)] * 2
    specs, shapes = [VMEM] * len(lefts), [(4, HALF, S, S), (4, W, S, S) if site else (4, 4, S, S)]
    scratch.append(pltpu.SemaphoreType.DMA((2 * N_CUT + 6 if site else 2,)))
    if site == 0:
        specs = [HBM] + [VMEM] * N_CUT
    out_specs = [VMEM, HBM if site else VMEM]
    return call(q_kernel, site, 4, specs, shapes, scratch, Q_FLOPS, sizes, lefts, amps, ops, after, out_specs)


def fetch_last(sizes, env):
    def body(sizes, env, out, sem):
        copy = pltpu.make_async_copy(env.at[place(sizes)[0] - 1], out, sem)
        copy.start()
        copy.wait()

    return pl.pallas_call(
        body,
        in_specs=[pl.BlockSpec(memory_space=pltpu.SMEM), HBM],
        out_specs=VMEM,
        scratch_shapes=[pltpu.SemaphoreType.DMA],
        out_shape=jax.ShapeDtypeStruct((W, S, S), BF16),
        compiler_params=pltpu.CompilerParams(vmem_limit_bytes=52 * MIB),
        name="fetch_last",
    )(sizes, env)


def finish(written, zero, zero_oth, rest_oth):
    def body(written, *refs):
        own, other, rest = refs[:N_CUT], refs[N_CUT : 2 * N_CUT], refs[2 * N_CUT : 2 * N_CUT + 3]
        out, sems = refs[2 * N_CUT + 3 :]

        @pl.when(lax.axis_index("site") == 1)
        def _():
            copies = []

            def add(ref, slot, v, length):
                copies.append(pltpu.make_async_copy(ref, out.at[slot, v : v + length], sems.at[len(copies)]))

            for k in range(3):
                add(rest[k], k + 1, 0, HALF)
            for half, parts in enumerate((other, own)):
                for (a, b), ref in zip(CUTS, parts):
                    add(ref, 0, half * HALF + a, b - a)
            start_all(copies)
            wait_all(copies)

    return pl.pallas_call(
        body,
        in_specs=[HBM] + [VMEM] * (2 * N_CUT + 3),
        out_specs=HBM,
        scratch_shapes=[pltpu.SemaphoreType.DMA((2 * N_CUT + 3,))],
        out_shape=jax.ShapeDtypeStruct((4, W, S, S), BF16),
        input_output_aliases={0: 0},
        compiler_params=pltpu.CompilerParams(vmem_limit_bytes=4 * MIB),
        name="finish",
    )(written, *zero, *zero_oth, *rest_oth)


def operator_blocks(weight, mask):
    kept = jnp.where(mask[:, None, None, :] != 0, weight, jnp.zeros_like(weight))
    return jnp.transpose(kept, (1, 2, 0, 3))


def later(x, *others):
    return lax.optimization_barrier((x, *others))[0]


def plus(x, y, take):
    return (x.astype(F32) + jnp.where(take, y.astype(F32), 0.0)).astype(BF16)


def shards(owners, environment, amplitudes, mpo_weight, mpo_mask, sector_count):
    owner = lax.axis_index("sector")
    across = [(c * owners + o, (1 - c) * owners + o) for c in range(2) for o in range(owners)]
    ahead = [(c * owners + o, c * owners + (o + 1) % owners) for c in range(2) for o in range(owners)]

    def swap(x):
        return lax.ppermute(x, AXES, across)

    def onward(x):
        return lax.ppermute(x, AXES, ahead)

    def final_onward(x):
        return lax.ppermute(x, AXES, [pair for pair in ahead if pair[1] % owners > 0])

    env = jnp.transpose(environment, (0, 2, 1, 3))
    own_ops = operator_blocks(mpo_weight[0], mpo_mask[0])
    amps = (amplitudes[0], swap(amplitudes[0]))
    ops = (own_ops, swap(own_ops))

    env_last = fetch_last(sector_count, env)
    edge_left, back_left, lefts = (env_last,), (env_last, env), (env,)
    inward = owner > 0
    for site in range(2):
        y_out = edge_two(site, sector_count, edge_left, amps, ops)
        y_in = [(final_onward if k == OPEN else onward)(y) for k, y in enumerate(y_out)]
        if site == 0:
            count = lax.dynamic_index_in_dim(later(sector_count, y_out[0]), owner, 0, keepdims=False)
            pass_on = jnp.logical_and(count == 1, inward)
        x_out = edge_one(site, sector_count, back_left, amps, ops, y_out)
        x_sent = [plus(x, y, pass_on) for x, y in zip(x_out, y_in)]
        x_in = [(final_onward if k == OPEN else onward)(x) for k, x in enumerate(x_sent)]
        made = inner(site, sector_count, (*lefts, *y_in), amps, ops, x_sent)
        inside = made[0]
        rest = [inside[k] for k in (1, 2, 3)]
        rest_oth = [swap(later(part, y_in[-1])) for part in rest]
        zero = [plus(later(inside, x)[0, a:b], x, inward) for (a, b), x in zip(CUTS, x_in)]
        if site == 0:
            zero_oth = [swap(block) for block in zero]
            lefts = edge_left = back_left = (*zero, *zero_oth, *rest, *rest_oth)
            amps = (made[1],)
        else:
            zero_oth = [swap(block) for block in zero]
            result = finish(made[1], zero, zero_oth, rest_oth)
    return jnp.transpose(result, (0, 2, 1, 3))[None]


def solution(mesh):
    placed = (
        P("sector", None, None, None),
        P("site", "sector", None, None, None),
        P("site", None, None, None, None),
        P("site", None, None),
        P(),
    )
    return jax.shard_map(
        functools.partial(shards, mesh.shape["sector"]),
        mesh=mesh,
        in_specs=placed,
        out_specs=P("site", "sector", None, None, None),
        check_vma=False,
    )
```

```python
import functools

import jax
import jax.numpy as jnp
from jax import lax
from jax.experimental import pallas as pl
from jax.experimental.pallas import tpu as pltpu
from jax.sharding import PartitionSpec as P

S = 128
W = 30
HALF = 15
CUTS = ((0, 8), (8, HALF))
Q_FLOPS = 8_000_000_000
OPEN = 0
N_CUT = len(CUTS)
AXES = ("site", "sector")
F32 = jnp.float32
BF16 = jnp.bfloat16
MIB = 1024 * 1024
HBM = pl.BlockSpec(memory_space=pltpu.HBM)
VMEM = pl.BlockSpec(memory_space=pltpu.VMEM)
ANY = pl.BlockSpec(memory_space=pl.ANY)


def iota(shape, dim):
    return lax.broadcasted_iota(jnp.int32, shape, dim)


def place(sizes):
    owner = lax.axis_index("sector")
    return sizes[owner], lax.axis_index("site"), owner


def expand_operator(core, site, states, w_own, w_oth, wk):
    row_v = iota((8 * HALF, W), 0) // 8 + core * HALF
    pick_v = (row_v == iota((8 * HALF, W), 1)).astype(BF16)
    spot = iota((W, 8 * W), 1) // 8
    if site:
        spot = jnp.where(core == 0, spot, jnp.where(spot < HALF, spot + HALF, spot - HALF))
    pick_w = (spot == iota((W, 8 * W), 0)).astype(BF16)
    diagonal = (iota((8 * HALF, 8 * W), 0) % 8) == (iota((8 * HALF, 8 * W), 1) % 8)

    def block(s, s2):
        chosen = jnp.where(core == site, w_own[s, s2].astype(F32), w_oth[s, s2].astype(F32)).astype(BF16)
        rows = lax.dot_general(pick_v, chosen, (((1,), (1,)), ((), ())), preferred_element_type=F32).astype(BF16)
        full = jnp.dot(rows, pick_w, preferred_element_type=F32)
        return jnp.where(diagonal, full, 0.0).astype(BF16)

    if 0 in states:
        wk[0][0] = block(0, 0)
    if 3 in states:
        wk[0][1] = block(3, 3)
    if 1 in states:
        upper = jnp.concatenate([block(1, 1), block(1, 2)], axis=1)
        lower = jnp.concatenate([block(2, 1), block(2, 2)], axis=1)
        wk[1][...] = jnp.concatenate([upper, lower], axis=0)


def first_steps(left, amps, states, wk, z):
    columns = jnp.concatenate([amps[s] for s in states], axis=1) if len(states) > 1 else amps[states[0]]
    rights = []
    for g in range(8):
        block = left[:, 16 * g : 16 * g + 16, :].reshape(W * 16, S)
        c = jnp.dot(block, columns, preferred_element_type=F32)
        c = c.reshape(W, 16, S * len(states))
        low = c[:, :8, :].reshape(W * 8, S * len(states)).astype(BF16)
        high = c[:, 8:, :].reshape(W * 8, S * len(states)).astype(BF16)
        rights.append(
            {
                s: jnp.concatenate([low[:, S * k : S * k + S], high[:, S * k : S * k + S]], axis=1)
                for k, s in enumerate(states)
            }
        )

    def keep(s, g, total):
        total = total.reshape(HALF, 8, 2 * S)
        z[s, :, 16 * g : 16 * g + 16, :] = jnp.concatenate([total[:, :, :S], total[:, :, S:]], axis=1).astype(BF16)

    for g in range(8):
        for s, p in ((0, 0), (3, 1)):
            if s in states:
                keep(s, g, jnp.dot(wk[0][p], rights[g][s], preferred_element_type=F32))
        if 1 in states:
            both = jnp.concatenate([rights[g][1], rights[g][2]], axis=0)
            total = jnp.dot(wk[1][...], both, preferred_element_type=F32)
            keep(1, g, total[: 8 * HALF])
            keep(2, g, total[8 * HALF :])


def last_step(amps, states, z, sink):
    turned = [amps[s].astype(F32).T.astype(BF16) for s in states]
    lhs = jnp.concatenate(turned, axis=1) if len(states) > 1 else turned[0]

    def right(v):
        return jnp.concatenate([z[s, v] for s in states], axis=0) if len(states) > 1 else z[states[0], v]

    for v in range(0, HALF, 2):
        count = min(2, HALF - v)
        rhs = jnp.concatenate([right(v), right(v + 1)], axis=1) if count > 1 else right(v)
        out = jnp.dot(lhs, rhs, preferred_element_type=F32)
        for i in range(count):
            sink(v + i, out[:, S * i : S * i + S])


def form_left(slot, left, refs):
    @pl.when(slot == 0)
    def _():
        for half in range(2):
            for (a, b), ref in zip(CUTS, refs[0][half]):
                left[half * HALF + a : half * HALF + b] = ref[...]

    for k in (1, 2, 3):
        @pl.when(slot == k)
        def _(k=k):
            for half in range(2):
                left[half * HALF : half * HALF + HALF] = refs[k][half][...]


def grouped(refs):
    rest = refs[2 * N_CUT :]
    return ((refs[:N_CUT], refs[N_CUT : 2 * N_CUT]), *((rest[k], rest[3 + k]) for k in range(3)))


def pick_amp(core, site, amp_refs, slot, s):
    if site:
        return amp_refs[0][slot, s]
    return jnp.where(core == site, amp_refs[0][slot, s].astype(F32), amp_refs[1][slot, s].astype(F32)).astype(BF16)


def y_kernel(site, sizes, lefts, amp_refs, w_own, w_oth, outs, left, wk, z):
    count, core, _ = place(sizes)
    slot = count - 1
    expand_operator(core, site, (3,), w_own, w_oth, wk)
    amps = {3: pick_amp(core, site, amp_refs, slot, 3)}
    if site:
        form_left(slot, left, grouped(lefts))
    first_steps(left if site else lefts[0], amps, (3,), wk, z)

    def sink(v, block):
        for (a, b), out in zip(CUTS, outs):
            if a <= v < b:
                out[v - a] = block.astype(BF16)

    last_step(amps, (3,), z, sink)


def x_kernel(site, sizes, lefts, amp_refs, w_own, w_oth, outs, left, wk, z, acc, *sems):
    count, core, _ = place(sizes)
    prior = jnp.maximum(count - 2, 0)
    if site == 0:
        fetch = pltpu.make_async_copy(lefts[1].at[prior], left, sems[0])
        fetch.start()
    expand_operator(core, site, (1, 2, 3), w_own, w_oth, wk)
    if site:
        form_left(count - 1, left, grouped(lefts))
    amps = {s: pick_amp(core, site, amp_refs, count - 1, s) for s in (1, 2)}
    first_steps(left if site else lefts[0], amps, (1, 2), wk, z)

    def put(read):
        def sink(v, block):
            for (a, b), out in zip(CUTS, outs):
                if a <= v < b:
                    out[v - a] = read(v, block).astype(BF16)

        return sink

    def keep(v, block):
        acc[v] = block

    last_step(amps, (1, 2), z, keep)
    if site == 0:
        fetch.wait()

    @pl.when(count >= 2)
    def _():
        if site:
            form_left(prior, left, grouped(lefts))
        amps = {3: pick_amp(core, site, amp_refs, prior, 3)}
        first_steps(left, amps, (3,), wk, z)
        last_step(amps, (3,), z, put(lambda v, block: acc[v] + block))

    @pl.when(count < 2)
    def _():
        for (a, b), out in zip(CUTS, outs):
            out[...] = acc[a:b].astype(BF16)


def q_kernel(site, sizes, lefts, amp_refs, w_own, w_oth, outs, left, wk, z, next_one, next_two, *sems):
    out = outs[0]
    lefts, y_refs = lefts[:-N_CUT], lefts[-N_CUT:]
    count, core, owner = place(sizes)
    step = pl.program_id(0)

    def fetch(slot):
        return pltpu.make_async_copy(lefts[0].at[slot], left.at[slot % 2], sems[0].at[slot % 2])

    @pl.when(step == 0)
    def _():
        if site == 0:
            fetch(0).start()
        else:
            pl.when(core == 0)(lambda: start_all(known_blocks(lefts, outs[1], sems[0])))
        expand_operator(core, site, (0, 1, 2, 3), w_own, w_oth, wk)
        next_one[...] = jnp.zeros_like(next_one)
        next_two[...] = jnp.zeros_like(next_two)

    if site == 0:
        @pl.when(step + 1 < count)
        def _():
            fetch(step + 1).start()

        for s in range(4):
            later_amp = jnp.where(core == 1, amp_refs[0][step, s].astype(F32), amp_refs[1][step, s].astype(F32))
            outs[1][step, s] = later_amp.astype(BF16)

        @pl.when(step < count)
        def _():
            fetch(step).wait()

        source = left.at[step % 2]
    else:
        @pl.when(step < count)
        def _():
            form_left(step, left, grouped(lefts))

        source = left

    @pl.when(jnp.logical_and(step == 1, owner > 0))
    def _():
        for (a, b), ref in zip(CUTS, y_refs):
            next_one[a:b] = next_one[a:b] + ref[...].astype(F32)

    def sink_zero(v, block):
        out[step, v] = (block + next_one[v]).astype(BF16)

    def sink_one(v, block):
        next_one[v] = block + next_two[v]

    def sink_two(v, block):
        next_two[v] = block

    def work(states):
        amps = {s: pick_amp(core, site, amp_refs, step, s) for s in states}
        first_steps(source, amps, states, wk, z)
        last_step(amps, (0,), z, sink_zero)
        if 1 in states:
            last_step(amps, (1, 2), z, sink_one)
        if 3 in states:
            last_step(amps, (3,), z, sink_two)

    @pl.when(step < count - 2)
    def _():
        work((0, 3, 1, 2))

    @pl.when(jnp.logical_and(step == count - 2, step >= 0))
    def _():
        work((0, 1, 2))

    @pl.when(step == count - 1)
    def _():
        work((0,))

    @pl.when(step >= count)
    def _():
        out[step] = jnp.zeros((HALF, S, S), BF16)

    if site:
        def own_half():
            return [pltpu.make_async_copy(out.at[k], outs[1].at[k, HALF:], sems[0].at[k - 1]) for k in (1, 2, 3)]

        @pl.when(step == 3)
        def _():
            pl.when(core == 0)(lambda: wait_all(known_blocks(lefts, outs[1], sems[0])))

            @pl.when(core == 1)
            def _():
                start_all(own_half())
                wait_all(own_half())


def start_all(copies):
    for copy in copies:
        copy.start()


def wait_all(copies):
    for copy in copies:
        copy.wait()


def known_blocks(lefts, out, sems):
    copies = []

    def add(ref, slot, v, length):
        copies.append(pltpu.make_async_copy(ref, out.at[slot, v : v + length], sems.at[len(copies)]))

    blocks = grouped(lefts)
    for half in range(2):
        for (a, b), ref in zip(CUTS, blocks[0][half]):
            add(ref, 0, half * HALF + a, b - a)
        for slot in (1, 2, 3):
            add(blocks[slot][half], slot, half * HALF, HALF)
    return copies


CUT_SHAPES = [(b - a, S, S) for a, b in CUTS]


def call(kernel, site, grid, left_specs, shapes, scratch, flops, sizes, lefts, amps, ops, after=(), out_specs=None):
    n_left, n_out, n_after, n_amp = len(lefts), len(shapes), len(after), len(amps)

    def body(sizes, *refs):
        left_refs, refs = refs[:n_left], refs[n_left:]
        amp_refs, op_refs, refs = refs[:n_amp], refs[n_amp : n_amp + 2], refs[n_amp + 2 + n_after :]
        left, wk_single, wk_pair, *others = refs[n_out:]
        kernel(site, sizes, left_refs, amp_refs, *op_refs, refs[:n_out], left, (wk_single, wk_pair), *others)

    return pl.pallas_call(
        body,
        grid_spec=pltpu.PrefetchScalarGridSpec(
            num_scalar_prefetch=1,
            grid=(grid,),
            in_specs=left_specs + [VMEM] * (n_amp + 2) + [ANY] * n_after,
            out_specs=out_specs or [VMEM] * n_out,
            scratch_shapes=scratch,
        ),
        out_shape=[jax.ShapeDtypeStruct(shape, BF16) for shape in shapes],
        cost_estimate=pl.CostEstimate(flops=flops, bytes_accessed=4_000_000, transcendentals=0),
        compiler_params=pltpu.CompilerParams(vmem_limit_bytes=(46 if kernel is q_kernel and site == 0 else 24) * MIB, dimension_semantics=("arbitrary",)),
        name=kernel.__name__ + str(site),
    )(sizes, *lefts, *amps, *ops, *after)


def work_space():
    return [pltpu.VMEM((2, 8 * HALF, 8 * W), BF16), pltpu.VMEM((16 * HALF, 16 * W), BF16), pltpu.VMEM((4, HALF, S, S), BF16)]


def edge_two(site, sizes, lefts, amps, ops):
    left = pltpu.VMEM((W, S, S) if site else (1, 8, S), BF16)
    return call(
        y_kernel, site, 1, [VMEM] * len(lefts), CUT_SHAPES, [left] + work_space(), 2_000_000_000, sizes, lefts, amps, ops
    )


def edge_one(site, sizes, lefts, amps, ops, after):
    scratch = [pltpu.VMEM((W, S, S), BF16)] + work_space() + [pltpu.VMEM((HALF, S, S), F32)]
    specs = [VMEM] * len(lefts)
    if site == 0:
        scratch.append(pltpu.SemaphoreType.DMA)
        specs = [VMEM, HBM]
    return call(x_kernel, site, 1, specs, CUT_SHAPES, scratch, 4_000_000_000, sizes, lefts, amps, ops, after)


def inner(site, sizes, lefts, amps, ops, after):
    left = pltpu.VMEM((W, S, S) if site else (2, W, S, S), BF16)
    scratch = [left] + work_space() + [pltpu.VMEM((HALF, S, S), F32)] * 2
    specs, shapes = [VMEM] * len(lefts), [(4, HALF, S, S), (4, W, S, S) if site else (4, 4, S, S)]
    scratch.append(pltpu.SemaphoreType.DMA((2 * N_CUT + 6 if site else 2,)))
    if site == 0:
        specs = [HBM] + [VMEM] * N_CUT
    out_specs = [VMEM, HBM if site else VMEM]
    return call(q_kernel, site, 4, specs, shapes, scratch, Q_FLOPS, sizes, lefts, amps, ops, after, out_specs)


def fetch_last(sizes, env):
    def body(sizes, env, out, sem):
        copy = pltpu.make_async_copy(env.at[place(sizes)[0] - 1], out, sem)
        copy.start()
        copy.wait()

    return pl.pallas_call(
        body,
        in_specs=[pl.BlockSpec(memory_space=pltpu.SMEM), HBM],
        out_specs=VMEM,
        scratch_shapes=[pltpu.SemaphoreType.DMA],
        out_shape=jax.ShapeDtypeStruct((W, S, S), BF16),
        compiler_params=pltpu.CompilerParams(vmem_limit_bytes=52 * MIB),
        name="fetch_last",
    )(sizes, env)


def finish(written, zero, zero_oth, rest_oth):
    def body(written, *refs):
        own, other, rest = refs[:N_CUT], refs[N_CUT : 2 * N_CUT], refs[2 * N_CUT : 2 * N_CUT + 3]
        out, sems = refs[2 * N_CUT + 3 :]

        @pl.when(lax.axis_index("site") == 1)
        def _():
            copies = []

            def add(ref, slot, v, length):
                copies.append(pltpu.make_async_copy(ref, out.at[slot, v : v + length], sems.at[len(copies)]))

            for k in range(3):
                add(rest[k], k + 1, 0, HALF)
            for half, parts in enumerate((other, own)):
                for (a, b), ref in zip(CUTS, parts):
                    add(ref, 0, half * HALF + a, b - a)
            start_all(copies)
            wait_all(copies)

    return pl.pallas_call(
        body,
        in_specs=[HBM] + [VMEM] * (2 * N_CUT + 3),
        out_specs=HBM,
        scratch_shapes=[pltpu.SemaphoreType.DMA((2 * N_CUT + 3,))],
        out_shape=jax.ShapeDtypeStruct((4, W, S, S), BF16),
        input_output_aliases={0: 0},
        compiler_params=pltpu.CompilerParams(vmem_limit_bytes=4 * MIB),
        name="finish",
    )(written, *zero, *zero_oth, *rest_oth)


def operator_blocks(weight, mask):
    kept = jnp.where(mask[:, None, None, :] != 0, weight, jnp.zeros_like(weight))
    return jnp.transpose(kept, (1, 2, 0, 3))


def later(x, *others):
    return lax.optimization_barrier((x, *others))[0]


def plus(x, y, take):
    return (x.astype(F32) + jnp.where(take, y.astype(F32), 0.0)).astype(BF16)


def shards(owners, environment, amplitudes, mpo_weight, mpo_mask, sector_count):
    owner = lax.axis_index("sector")
    across = [(c * owners + o, (1 - c) * owners + o) for c in range(2) for o in range(owners)]
    ahead = [(c * owners + o, c * owners + (o + 1) % owners) for c in range(2) for o in range(owners)]

    def swap(x):
        return lax.ppermute(x, AXES, across)

    def onward(x):
        return lax.ppermute(x, AXES, ahead)

    def final_onward(x):
        return lax.ppermute(x, AXES, [pair for pair in ahead if pair[1] % owners > 0])

    env = jnp.transpose(environment, (0, 2, 1, 3))
    own_ops = operator_blocks(mpo_weight[0], mpo_mask[0])
    amps = (amplitudes[0], swap(amplitudes[0]))
    ops = (own_ops, swap(own_ops))

    env_last = fetch_last(sector_count, env)
    edge_left, back_left, lefts = (env_last,), (env_last, env), (env,)
    inward = owner > 0
    for site in range(2):
        y_out = edge_two(site, sector_count, edge_left, amps, ops)
        y_in = [(final_onward if k == OPEN else onward)(y) for k, y in enumerate(y_out)]
        if site == 0:
            count = lax.dynamic_index_in_dim(later(sector_count, y_out[0]), owner, 0, keepdims=False)
            pass_on = jnp.logical_and(count == 1, inward)
        x_out = edge_one(site, sector_count, back_left, amps, ops, y_out)
        x_sent = [plus(x, y, pass_on) for x, y in zip(x_out, y_in)]
        x_in = [(final_onward if k == OPEN else onward)(x) for k, x in enumerate(x_sent)]
        made = inner(site, sector_count, (*lefts, *y_in), amps, ops, x_sent)
        inside = made[0]
        rest = [inside[k] for k in (1, 2, 3)]
        rest_oth = [swap(later(part, y_in[-1])) for part in rest]
        zero = [plus(later(inside, x)[0, a:b], x, inward) for (a, b), x in zip(CUTS, x_in)]
        if site == 0:
            zero_oth = [swap(block) for block in zero]
            lefts = edge_left = back_left = (*zero, *zero_oth, *rest, *rest_oth)
            amps = (made[1],)
        else:
            zero_oth = [swap(block) for block in zero]
            result = finish(made[1], zero, zero_oth, rest_oth)
    return jnp.transpose(result, (0, 2, 1, 3))[None]


def solution(mesh):
    placed = (
        P("sector", None, None, None),
        P("site", "sector", None, None, None),
        P("site", None, None, None, None),
        P("site", None, None),
        P(),
    )
    return jax.shard_map(
        functools.partial(shards, mesh.shape["sector"]),
        mesh=mesh,
        in_specs=placed,
        out_specs=P("site", "sector", None, None, None),
        check_vma=False,
    )
```
